32 devices in a mesh: tm: 16 (over z, y, x), head: 2 (over core).
Axes of the slice: x: 2, y: 2, z: 4, core: 2. Of those that a mesh axis runs over, the one named last changes fastest.
Arguments:
- clean_qkv: bfloat16 [3, 8192, 5120], P(None, 'tm', 'head'), may hold values from -140 to 140
- noise_qkv: bfloat16 [3, 8192, 5120], P(None, 'tm', 'head'), may hold values from -140 to 140
- timestep: int32 [16], P('tm'), may hold values from 1 to 999
- gain_q: float32 [5120], P('head'), may hold values from 0.1 to 1.9
- gain_k: float32 [5120], P('head'), may hold values from 0.1 to 1.9
- attended_grad: bfloat16 [8192, 5120], P('tm', 'head'), may hold values from -6 to 6
Outputs:
- attended: bfloat16 [8192, 5120], P('tm', 'head')
- clean_grads: float32 [3, 8192, 5120], P(None, 'tm', 'head')
The draws below stay inside these ranges and needn't reach their ends.
All inputs are finite; a program needn't handle non-finite values.
Results may differ from the reference program's by a relative error of at most 0.012.
The reference program's roundings to bfloat16 on the way count: a program that leaves them out, or rounds other values in their place, can miss the bound.
Values may be sent and summed in bfloat16 or wider, within the bound.
A program may use at most 256 MiB of HBM per device.

```python
import math
import jax
import jax.numpy as jnp
from jax import lax

D = 5120
HEADS = 40
HEAD_DIM = 128
SPAN_ROWS = 512
CONTEXT = 3
SPANS = 16
TOKENS = 8192


def field_draw(key, tag):
    own_key = jax.random.fold_in(key, tag)
    value_key, scale_key = jax.random.split(own_key)
    token_key = jax.random.fold_in(own_key, 7)
    fields = jnp.clip(jax.random.normal(value_key, (3, TOKENS, D), jnp.float32), -6.0, 6.0)
    token_scale = jnp.exp(jax.random.uniform(token_key, (3, TOKENS, 1), jnp.float32) * math.log(10.0))
    head_scale = jnp.exp(jax.random.uniform(scale_key, (3, TOKENS, HEADS), jnp.float32) * math.log(1.2))
    fields = fields * token_scale * jnp.repeat(head_scale, HEAD_DIM, axis=2)
    return fields


def draw_clean_qkv(key, part):
    return field_draw(key, 1).astype(jnp.bfloat16)


def draw_noise_qkv(key, part):
    return field_draw(key, 2).astype(jnp.bfloat16)


def with_ends(drawn, key, least, largest):
    extent = drawn.shape
    spot = [jax.random.randint(jax.random.fold_in(key, axis), (), 0, extent[axis]) for axis in range(len(extent))]
    drawn = drawn.at[tuple(spot)].set(least)
    longest = extent.index(max(extent))
    spot[longest] = (spot[longest] + 1) % extent[longest]
    return drawn.at[tuple(spot)].set(largest)


def block_scale(rng, extent, pieces, smallest, high):
    loudness, own = 1.0, jax.random.fold_in(rng, 6)
    for position, blocks in pieces:
        steps = jnp.exp(jax.random.uniform(jax.random.fold_in(own, position), (blocks,), jnp.float32, smallest / len(pieces), high / len(pieces)))
        loudness = loudness * jnp.repeat(steps, extent[position] // blocks).reshape([-1 if axis == position else 1 for axis in range(len(extent))])
    return loudness


def scatter_about(stream_key, extent, scale, reach, cuts=(), kind=jnp.bfloat16):
    drawn = jax.random.normal(stream_key, extent, jnp.float32) * scale
    if len(cuts) > 0:
        drawn = block_scale(stream_key, extent, cuts, -0.22, 0.18) * drawn
    return jnp.clip(drawn, min=-reach, max=reach).astype(kind)


def setup_inputs(seed: int = 0) -> dict:
    seeds = jax.random.split(jax.random.key(seed), 7)
    return {
        "clean_qkv": draw_clean_qkv(jax.random.fold_in(seeds[6], 71), 0),
        "noise_qkv": draw_noise_qkv(jax.random.fold_in(seeds[6], 71), 0),
        "timestep": with_ends(jax.random.randint(seeds[2], (SPANS,), 1, 1000), jax.random.fold_in(seeds[2], 1), 1, 999).astype(jnp.int32),
        "gain_q": jnp.clip(1.0 + 0.18 * jax.random.normal(seeds[3], (D,), jnp.float32), 0.1, 1.9),
        "gain_k": jnp.clip(1.0 + 0.18 * jax.random.normal(seeds[4], (D,), jnp.float32), 0.1, 1.9),
        "attended_grad": scatter_about(seeds[5], (TOKENS, D), 1.0, 6.0, ((0, 16), (1, 2))),
    }


epsilon = 1e-06
masked_score = -1e+30

def noise_share_of(timestep):
    level = timestep.astype(jnp.float32) / 1000.0
    return 5.0 * level / (1.0 + 4.0 * level)

def inverse_rms(field):
    return lax.rsqrt(lax.optimization_barrier(jnp.mean(field * field, axis=-1, keepdims=True)) + epsilon)

def norm_backward(field, inverse, gain, grad):
    inner = lax.optimization_barrier(jnp.mean(field * gain * grad, axis=-1, keepdims=True))
    return inverse * gain * grad - field * inverse ** 3 * inner

def reference(clean_qkv, noise_qkv, timestep, gain_q, gain_k, attended_grad):
    highest = lax.Precision.HIGHEST
    noise_all = noise_share_of(timestep)
    clean_key_pre = clean_qkv[1].astype(jnp.float32)
    key_clean_all = (clean_key_pre * inverse_rms(clean_key_pre) * gain_k).astype(jnp.bfloat16)
    value_clean_all = clean_qkv[2]
    score_scale = HEAD_DIM ** (-0.5)

    def span_step(carried_state, span_index):
        pending_keys, pending_values = carried_state
        first_row = (span_index * SPAN_ROWS).astype(jnp.int32)
        noise_share = noise_all[span_index]
        keep_share = 1.0 - noise_share
        clean_field = lax.dynamic_slice_in_dim(clean_qkv, first_row, SPAN_ROWS, 1).astype(jnp.float32)
        noise_field = lax.dynamic_slice_in_dim(noise_qkv, first_row, SPAN_ROWS, 1).astype(jnp.float32)
        noisy_field = keep_share * clean_field + noise_share * noise_field
        inverse_query = inverse_rms(noisy_field[0])
        inverse_key = inverse_rms(noisy_field[1])
        inverse_clean = inverse_rms(clean_field[1])
        query_rows = (noisy_field[0] * inverse_query * gain_q).astype(jnp.bfloat16)
        key_own = (noisy_field[1] * inverse_key * gain_k).astype(jnp.bfloat16)
        value_own = noisy_field[2].astype(jnp.bfloat16)
        key_parts = [key_own]
        value_parts = [value_own]
        valid_parts = [jnp.ones((SPAN_ROWS,), dtype=bool)]
        for hop_index in range(1, CONTEXT + 1):
            source_row = (jnp.maximum(span_index - hop_index, 0) * SPAN_ROWS).astype(jnp.int32)
            key_parts.append(lax.dynamic_slice_in_dim(key_clean_all, source_row, SPAN_ROWS, 0))
            value_parts.append(lax.dynamic_slice_in_dim(value_clean_all, source_row, SPAN_ROWS, 0))
            valid_parts.append(jnp.full((SPAN_ROWS,), span_index >= hop_index))
        key_rows = jnp.concatenate(key_parts, axis=0)
        value_rows = jnp.concatenate(value_parts, axis=0)
        key_valid = jnp.concatenate(valid_parts, axis=0)
        query_cube = query_rows.astype(jnp.float32).reshape(SPAN_ROWS, HEADS, HEAD_DIM)
        key_cube = key_rows.astype(jnp.float32).reshape(-1, HEADS, HEAD_DIM)
        value_cube = value_rows.astype(jnp.float32).reshape(-1, HEADS, HEAD_DIM)
        grad_rows = lax.dynamic_slice_in_dim(attended_grad, first_row, SPAN_ROWS, 0)
        grad_cube = grad_rows.astype(jnp.float32).reshape(SPAN_ROWS, HEADS, HEAD_DIM)
        scores = jnp.einsum('qhd,khd->hqk', query_cube, key_cube, precision=highest) * score_scale
        scores = jnp.where(key_valid[None, None, :], scores, masked_score)
        row_max = lax.optimization_barrier(jnp.max(scores, axis=-1, keepdims=True))
        exponent = jnp.exp(scores - row_max)
        attention = exponent / lax.optimization_barrier(jnp.sum(exponent, axis=-1, keepdims=True))
        weights = lax.optimization_barrier(attention.astype(jnp.bfloat16)).astype(jnp.float32)
        output_rows = jnp.einsum('hqk,khd->qhd', weights, value_cube, precision=highest)
        output_rows = output_rows.reshape(SPAN_ROWS, D).astype(jnp.bfloat16)
        grad_probs = jnp.einsum('qhd,khd->hqk', grad_cube, value_cube, precision=highest)
        row_delta = lax.optimization_barrier(jnp.sum(attention * grad_probs, axis=-1, keepdims=True))
        grad_scores = (attention * (grad_probs - row_delta) * score_scale).astype(jnp.bfloat16)
        grad_scores = lax.optimization_barrier(grad_scores).astype(jnp.float32)
        grad_query = jnp.einsum('hqk,khd->qhd', grad_scores, key_cube, precision=highest).reshape(SPAN_ROWS, D)
        grad_keys = jnp.einsum('hqk,qhd->khd', grad_scores, query_cube, precision=highest).reshape(-1, D)
        grad_values = jnp.einsum('hqk,qhd->khd', weights, grad_cube, precision=highest).reshape(-1, D)
        grad_query_pre = norm_backward(noisy_field[0], inverse_query, gain_q, grad_query)
        grad_own_pre = norm_backward(noisy_field[1], inverse_key, gain_k, grad_keys[:SPAN_ROWS])
        grad_clean_pre = norm_backward(clean_field[1], inverse_clean, gain_k, pending_keys[0])
        clean_grads = jnp.stack([keep_share * grad_query_pre, keep_share * grad_own_pre + grad_clean_pre, keep_share * grad_values[:SPAN_ROWS] + pending_values[0]])
        next_keys = []
        next_values = []
        for hop_index in range(CONTEXT - 1):
            lower = (hop_index + 1) * SPAN_ROWS
            next_keys.append(pending_keys[hop_index + 1] + grad_keys[lower:lower + SPAN_ROWS])
            next_values.append(pending_values[hop_index + 1] + grad_values[lower:lower + SPAN_ROWS])
        next_keys.append(grad_keys[CONTEXT * SPAN_ROWS:])
        next_values.append(grad_values[CONTEXT * SPAN_ROWS:])
        return ((jnp.stack(next_keys), jnp.stack(next_values)), (output_rows, clean_grads))
    start_state = (jnp.zeros((CONTEXT, SPAN_ROWS, D), jnp.float32), jnp.zeros((CONTEXT, SPAN_ROWS, D), jnp.float32))
    final_state, results = lax.scan(span_step, start_state, jnp.arange(SPANS, dtype=jnp.int32), reverse=True)
    outputs, gradients = results
    attended = outputs.reshape(TOKENS, D)
    clean_grads = jnp.transpose(gradients, (1, 0, 2, 3)).reshape(3, TOKENS, D)
    return (attended, clean_grads)
```

```python
import functools
import jax
import jax.numpy as jnp
from jax import lax
from jax.experimental import pallas as pl
from jax.experimental.pallas import tpu as pltpu
from jax.sharding import PartitionSpec as P

D = 5120
HEAD_DIM = 128
CONTEXT = 3


epsilon = 1e-06
masked_score = -1e30


def from_behind(block, axis, distance):
    devices = range(lax.axis_size(axis))
    route = [(i - distance, i) for i in devices if i - distance in devices]
    return lax.ppermute(block, axis, route)


def noise_share_of(timestep):
    level = timestep.astype(jnp.float32) / 1000.0
    return 5.0 * level / (1.0 + 4.0 * level)


def contract(left, right, left_dim, right_dim):
    return lax.dot_general(
        left, right, (((left_dim,), (right_dim,)), ((), ())), preferred_element_type=jnp.float32
    )


def on_device(clean_qkv, noise_qkv, timestep, gain_q, gain_k, attended_grad):
    row_count = clean_qkv.shape[1]
    local_width = clean_qkv.shape[2]
    heads_here = local_width // HEAD_DIM
    span_index = lax.axis_index("tm")
    noise_share = noise_share_of(timestep[0])
    keep_share = 1.0 - noise_share
    clean_field = clean_qkv.astype(jnp.float32)
    noisy_field = keep_share * clean_field + noise_share * noise_qkv.astype(jnp.float32)
    partial_sums = jnp.stack(
        [
            jnp.sum(noisy_field[0] * noisy_field[0], axis=-1),
            jnp.sum(noisy_field[1] * noisy_field[1], axis=-1),
            jnp.sum(clean_field[1] * clean_field[1], axis=-1),
        ]
    )
    totals = lax.psum(partial_sums, "head")
    inverse = lax.rsqrt(totals / D + epsilon)
    query_rows = (noisy_field[0] * inverse[0][:, None] * gain_q).astype(jnp.bfloat16)
    key_own = (noisy_field[1] * inverse[1][:, None] * gain_k).astype(jnp.bfloat16)
    key_clean = (clean_field[1] * inverse[2][:, None] * gain_k).astype(jnp.bfloat16)
    value_own = noisy_field[2].astype(jnp.bfloat16)
    value_clean = clean_qkv[2]
    outgoing = jnp.stack([key_clean, value_clean])
    arrived = []
    for hop_index in range(CONTEXT):
        arrived.append(from_behind(outgoing, "tm", hop_index + 1))
    key_rows = jnp.concatenate([key_own] + [piece[0] for piece in arrived], axis=0)
    value_rows = jnp.concatenate([value_own] + [piece[1] for piece in arrived], axis=0)
    block_ids = jnp.arange(CONTEXT + 1, dtype=jnp.int32)
    block_valid = span_index >= block_ids
    key_valid = jnp.repeat(block_valid, row_count)
    score_scale = HEAD_DIM ** (-0.5)
    key_count = (CONTEXT + 1) * row_count

    def one_head(head_index, carried_state):
        output_acc, query_acc, keys_acc, values_acc, stat_acc = carried_state
        head_start = head_index * HEAD_DIM
        query_head = lax.dynamic_slice_in_dim(query_rows, head_start, HEAD_DIM, 1)
        key_head = lax.dynamic_slice_in_dim(key_rows, head_start, HEAD_DIM, 1)
        value_head = lax.dynamic_slice_in_dim(value_rows, head_start, HEAD_DIM, 1)
        grad_head = lax.dynamic_slice_in_dim(attended_grad, head_start, HEAD_DIM, 1)
        scores = contract(query_head, key_head, 1, 1) * score_scale
        scores = jnp.where(key_valid[None, :], scores, masked_score)
        row_max = jnp.max(scores, axis=-1, keepdims=True)
        exponent = jnp.exp(scores - row_max)
        row_total = jnp.sum(exponent, axis=-1, keepdims=True)
        attention = exponent / row_total
        weights = attention.astype(jnp.bfloat16)
        output_head = jnp.dot(weights, value_head, preferred_element_type=jnp.float32)
        grad_probs = contract(grad_head, value_head, 1, 1)
        row_delta = jnp.sum(attention * grad_probs, axis=-1, keepdims=True)
        grad_scores = (attention * (grad_probs - row_delta) * score_scale).astype(jnp.bfloat16)
        grad_query_head = jnp.dot(grad_scores, key_head, preferred_element_type=jnp.float32)
        grad_key_head = contract(grad_scores, query_head, 0, 0)
        grad_value_head = contract(weights, grad_head, 0, 0)
        head_stats = jnp.stack([row_max[:, 0], row_total[:, 0], row_delta[:, 0]])[:, None, :]
        output_acc = lax.dynamic_update_slice_in_dim(output_acc, output_head, head_start, 1)
        query_acc = lax.dynamic_update_slice_in_dim(query_acc, grad_query_head, head_start, 1)
        keys_acc = lax.dynamic_update_slice_in_dim(keys_acc, grad_key_head, head_start, 1)
        values_acc = lax.dynamic_update_slice_in_dim(values_acc, grad_value_head, head_start, 1)
        stat_acc = lax.dynamic_update_slice_in_dim(stat_acc, head_stats, head_index, 1)
        return (output_acc, query_acc, keys_acc, values_acc, stat_acc)

    start_state = (
        jnp.zeros((row_count, local_width), jnp.float32),
        jnp.zeros((row_count, local_width), jnp.float32),
        jnp.zeros((key_count, local_width), jnp.float32),
        jnp.zeros((key_count, local_width), jnp.float32),
        jnp.zeros((3, heads_here, row_count), jnp.float32),
    )
    output_acc, grad_query, grad_keys, grad_values, row_stats = lax.fori_loop(
        0, heads_here, one_head, start_state
    )
    attended = output_acc.astype(jnp.bfloat16)
    returns_parts = []
    for hop_index in range(1, CONTEXT + 1):
        lower = hop_index * row_count
        returns_parts.append(
            jnp.stack(
                [grad_keys[lower : lower + row_count], grad_values[lower : lower + row_count]]
            )
        )
    context_grads = jnp.zeros_like(returns_parts[0])
    for hop_index in range(CONTEXT):
        context_grads = context_grads + from_behind(
            returns_parts[hop_index], "tm", -(hop_index + 1)
        )
    context_key_grad = context_grads[0]
    context_value_grad = context_grads[1]
    own_key_grad = grad_keys[:row_count]
    inner_sums = jnp.stack(
        [
            jnp.sum(noisy_field[0] * gain_q * grad_query, axis=-1),
            jnp.sum(noisy_field[1] * gain_k * own_key_grad, axis=-1),
            jnp.sum(clean_field[1] * gain_k * context_key_grad, axis=-1),
        ]
    )
    inner_totals = lax.psum(inner_sums, "head")
    cube_term = inverse**3 * inner_totals / D
    grad_query_pre = (
        inverse[0][:, None] * gain_q * grad_query - noisy_field[0] * cube_term[0][:, None]
    )
    grad_own_pre = (
        inverse[1][:, None] * gain_k * own_key_grad - noisy_field[1] * cube_term[1][:, None]
    )
    grad_clean_pre = (
        inverse[2][:, None] * gain_k * context_key_grad - clean_field[1] * cube_term[2][:, None]
    )
    clean_grads = jnp.stack(
        [
            keep_share * grad_query_pre,
            keep_share * grad_own_pre + grad_clean_pre,
            keep_share * grad_values[:row_count] + context_value_grad,
        ]
    )
    return (attended, clean_grads)


GROUP = 4
ROWS = 64
LOG2E = 1.4426950408889634
VMEM_LIMIT = 52 * 1024 * 1024


def chunks_of(heads):
    sizes = []
    while heads > 0:
        sizes.append(min(2, heads))
        heads -= sizes[-1]
    return sizes


def swap(block, distance):
    return lax.ppermute(block, "tm", [(i, i ^ distance) for i in range(lax.axis_size("tm"))])


def other_core(block):
    return lax.ppermute(block, "head", [(0, 1), (1, 0)])


def columns_at(place, width, offset, count):
    return pl.ds(pl.multiple_of(place * width + offset, HEAD_DIM), count)


def pack_lanes(parts):
    lane = lax.broadcasted_iota(jnp.int32, (parts[0].shape[0], 128), 1)
    packed = jnp.zeros((parts[0].shape[0], 128), jnp.float32)
    for index, part in enumerate(parts):
        packed = jnp.where(lane == index, part, packed)
    return packed


def values_kernel(width, place_ref, share_ref, clean_ref, noise_ref, grad_ref, sums_ref, *out_refs):
    keep, share = share_ref[0], share_ref[1]
    place = place_ref[0]
    squares = [0.0, 0.0, 0.0]
    for group in range(GROUP):
        cols = pl.ds(group * width, width)
        clean_key = clean_ref[1, :, cols].astype(jnp.float32)
        query = keep * clean_ref[0, :, cols].astype(jnp.float32) + share * noise_ref[0, :, cols].astype(jnp.float32)
        key = keep * clean_key + share * noise_ref[1, :, cols].astype(jnp.float32)
        for index, field in enumerate((query, key, clean_key)):
            squares[index] = squares[index] + jnp.sum(field * field, axis=-1, keepdims=True)
    sums_ref[...] = pack_lanes(squares)
    for distance in range(GROUP):
        cols = columns_at(place ^ distance, width, 0, width)
        clean = clean_ref[2, :, cols]
        noisy = keep * clean.astype(jnp.float32) + share * noise_ref[2, :, cols].astype(jnp.float32)
        out_refs[distance][0] = clean
        out_refs[distance][1] = noisy.astype(jnp.bfloat16)
        out_refs[distance][2] = grad_ref[:, cols]


def keys_kernel(width, sizes, place_ref, share_ref, clean_ref, noise_ref, gains_ref, sums_ref, other_ref, *out_refs):
    keep, share = share_ref[0], share_ref[1]
    place = place_ref[0]
    inverse = lax.rsqrt((sums_ref[...] + other_ref[...]) / D + epsilon)
    for distance in range(GROUP):
        offset = 0
        for chunk, heads in enumerate(sizes):
            count = heads * HEAD_DIM
            cols = columns_at(place ^ distance, width, offset, count)
            out_ref = out_refs[chunk * GROUP + distance]
            gain_q, gain_k = gains_ref[0:1, cols], gains_ref[1:2, cols]
            clean_key = clean_ref[1, :, cols].astype(jnp.float32)
            query = keep * clean_ref[0, :, cols].astype(jnp.float32) + share * noise_ref[0, :, cols].astype(jnp.float32)
            key = keep * clean_key + share * noise_ref[1, :, cols].astype(jnp.float32)
            out_ref[0] = (clean_key * inverse[:, 2:3] * gain_k).astype(jnp.bfloat16)
            out_ref[1] = (query * inverse[:, 0:1] * gain_q).astype(jnp.bfloat16)
            out_ref[2] = (key * inverse[:, 1:2] * gain_k).astype(jnp.bfloat16)
            offset += count


def attention_kernel(place_ref, keep_ref, *refs):
    value_refs, key_refs, halo_ref = refs[:4], refs[4:8], refs[8]
    back_refs, ctx_ref, halo_grad_ref = refs[9:13], refs[13], refs[14]
    keys, values, queries, own_keys, own_values, grads, back, key_acc, value_acc = refs[15:]
    place, first = place_ref[0], place_ref[1]
    scale = HEAD_DIM ** (-0.5)
    for distance in range(GROUP):
        spot = place ^ distance
        keys[spot] = halo_ref[GROUP + distance]
        values[spot] = halo_ref[distance]
        keys[GROUP + spot] = key_refs[distance][0]
        values[GROUP + spot] = value_refs[distance][0]
        queries[spot] = key_refs[distance][1]
        own_keys[spot] = key_refs[distance][2]
        own_values[spot] = value_refs[distance][1]
        grads[spot] = value_refs[distance][2]
    key_acc[...] = jnp.zeros_like(key_acc)
    value_acc[...] = jnp.zeros_like(value_acc)

    def one_span(span, carry):
        query, grad = queries[span], grads[span]
        slots = [span + GROUP - hop for hop in range(1, CONTEXT + 1)]
        key_blocks = [own_keys[span]] + [keys[slot] for slot in slots]
        value_blocks = [own_values[span]] + [values[slot] for slot in slots]
        absent = [0.0] + [
            jnp.where(jnp.logical_and(first == 1, slot < GROUP), -masked_score, 0.0) for slot in slots
        ]
        scores = [contract(block, query, 1, 1) * (scale * LOG2E) for block in key_blocks]
        top = functools.reduce(
            jnp.maximum,
            [jnp.max(part, axis=0, keepdims=True) - lack for part, lack in zip(scores, absent)],
        )
        exponents = [jnp.exp2(part - (top + lack)) for part, lack in zip(scores, absent)]
        total = sum(jnp.sum(part, axis=0, keepdims=True) for part in exponents)
        recip = 1.0 / total
        attention = [part * recip for part in exponents]
        weights = [part.astype(jnp.bfloat16) for part in attention]
        output = sum(contract(block, part, 0, 0) for block, part in zip(value_blocks, weights))
        grad_turned = jnp.transpose(grad.astype(jnp.float32))
        delta = jnp.sum(output * grad_turned, axis=0, keepdims=True)
        back[span, 0] = jnp.transpose(output).astype(jnp.bfloat16)
        grad_query = 0.0
        for index in range(CONTEXT + 1):
            probs = contract(value_blocks[index], grad, 1, 1)
            change = (attention[index] * (probs - delta) * scale).astype(jnp.bfloat16)
            grad_query = grad_query + contract(key_blocks[index], change, 0, 0)
            grad_key = jnp.dot(change, query, preferred_element_type=jnp.float32)
            grad_value = jnp.dot(weights[index], grad, preferred_element_type=jnp.float32)
            if index == 0:
                back[span, 2] = grad_key.astype(jnp.bfloat16)
                own_slot = GROUP + span
                value_acc[own_slot] = value_acc[own_slot] + keep_ref[span ^ place] * grad_value
            else:
                slot = slots[index - 1]
                key_acc[slot] = key_acc[slot] + grad_key
                value_acc[slot] = value_acc[slot] + grad_value
        back[span, 1] = jnp.transpose(grad_query).astype(jnp.bfloat16)
        return carry

    lax.fori_loop(0, GROUP, one_span, 0)
    for distance in range(GROUP):
        spot = place ^ distance
        back_refs[distance][...] = back[spot]
        ctx_ref[distance, 0] = key_acc[GROUP + spot]
        ctx_ref[distance, 1] = value_acc[GROUP + spot]
        halo_grad_ref[distance, 0] = key_acc[spot].astype(jnp.bfloat16)
        halo_grad_ref[distance, 1] = value_acc[spot].astype(jnp.bfloat16)


def noisy_at(clean_ref, noise_ref, index, cols, keep, share):
    return keep * clean_ref[index, :, cols].astype(jnp.float32) + share * noise_ref[index, :, cols].astype(jnp.float32)


def inner_kernel(width, sizes, place_ref, share_ref, clean_ref, noise_ref, gains_ref, *refs):
    pieces = len(sizes) * GROUP
    back_refs, ctx_refs = refs[:pieces], refs[pieces : 2 * pieces]
    attended_ref, inner_ref = refs[2 * pieces :]
    keep, share = share_ref[0], share_ref[1]
    place = place_ref[0]
    inner = [0.0, 0.0, 0.0]
    for distance in range(GROUP):
        offset = 0
        for chunk, heads in enumerate(sizes):
            count = heads * HEAD_DIM
            cols = columns_at(place ^ distance, width, offset, count)
            back_ref, ctx_ref = back_refs[chunk * GROUP + distance], ctx_refs[chunk * GROUP + distance]
            gain_q, gain_k = gains_ref[0:1, cols], gains_ref[1:2, cols]
            attended_ref[:, cols] = back_ref[0]
            terms = (
                noisy_at(clean_ref, noise_ref, 0, cols, keep, share) * gain_q * back_ref[1].astype(jnp.float32),
                noisy_at(clean_ref, noise_ref, 1, cols, keep, share) * gain_k * back_ref[2].astype(jnp.float32),
                clean_ref[1, :, cols].astype(jnp.float32) * gain_k * ctx_ref[0].astype(jnp.float32),
            )
            for index, term in enumerate(terms):
                inner[index] = inner[index] + jnp.sum(term, axis=-1, keepdims=True)
            offset += count
    inner_ref[...] = pack_lanes(inner)


def finish_kernel(
    width, sizes, place_ref, share_ref, clean_ref, noise_ref, gains_ref,
    sums_ref, sums_other_ref, inner_ref, inner_other_ref, *refs
):
    pieces = len(sizes) * GROUP
    back_refs, ctx_refs, grads_ref = refs[:pieces], refs[pieces : 2 * pieces], refs[2 * pieces]
    keep, share = share_ref[0], share_ref[1]
    place = place_ref[0]
    inverse = lax.rsqrt((sums_ref[...] + sums_other_ref[...]) / D + epsilon)
    cube = inverse * inverse * inverse * ((inner_ref[...] + inner_other_ref[...]) / D)
    for distance in range(GROUP):
        offset = 0
        for chunk, heads in enumerate(sizes):
            count = heads * HEAD_DIM
            cols = columns_at(place ^ distance, width, offset, count)
            back_ref, ctx_ref = back_refs[chunk * GROUP + distance], ctx_refs[chunk * GROUP + distance]
            gain_q, gain_k = gains_ref[0:1, cols], gains_ref[1:2, cols]
            query = noisy_at(clean_ref, noise_ref, 0, cols, keep, share)
            key = noisy_at(clean_ref, noise_ref, 1, cols, keep, share)
            clean_key = clean_ref[1, :, cols].astype(jnp.float32)
            grad_query = inverse[:, 0:1] * gain_q * back_ref[1].astype(jnp.float32) - query * cube[:, 0:1]
            grad_own = inverse[:, 1:2] * gain_k * back_ref[2].astype(jnp.float32) - key * cube[:, 1:2]
            grad_clean = inverse[:, 2:3] * gain_k * ctx_ref[0].astype(jnp.float32) - clean_key * cube[:, 2:3]
            grads_ref[0, :, cols] = keep * grad_query
            grads_ref[1, :, cols] = keep * grad_own + grad_clean
            grads_ref[2, :, cols] = ctx_ref[1].astype(jnp.float32)
            offset += count


def on_group(clean_qkv, noise_qkv, timestep, gain_q, gain_k, attended_grad):
    rows, local_width = clean_qkv.shape[1:]
    width = local_width // GROUP
    sizes = chunks_of(width // HEAD_DIM)
    tm = lax.axis_index("tm")
    group_count = lax.axis_size("tm") // GROUP
    place = lax.rem(tm, GROUP)
    first = (tm < GROUP).astype(jnp.int32)
    places = jnp.stack([place, first]).astype(jnp.int32)
    noise_share = noise_share_of(timestep[0])
    keep_share = 1.0 - noise_share
    shares = jnp.stack([keep_share, noise_share])
    gains = jnp.stack([gain_q, gain_k])
    keep_tile = jnp.full((8, 128), keep_share, jnp.float32)
    keeps = jnp.stack([keep_share] + [swap(keep_tile, d)[0, 0] for d in range(1, GROUP)])

    smem = pl.BlockSpec(memory_space=pltpu.SMEM)
    params = pltpu.CompilerParams(vmem_limit_bytes=VMEM_LIMIT)
    grid = (rows // ROWS,)

    def by_rows(parts, count):
        return pl.BlockSpec((parts, ROWS, count), lambda i: (0, i, 0))

    flat = lambda count: pl.BlockSpec((ROWS, count), lambda i: (i, 0))
    gain_spec = pl.BlockSpec((2, local_width), lambda i: (0, 0))

    def bf16(*shape):
        return jax.ShapeDtypeStruct(shape, jnp.bfloat16)

    sums, *values = pl.pallas_call(
        functools.partial(values_kernel, width),
        grid=grid,
        in_specs=[smem, smem, by_rows(3, local_width), by_rows(3, local_width), flat(local_width)],
        out_specs=[flat(128)] + [by_rows(3, width)] * GROUP,
        out_shape=[jax.ShapeDtypeStruct((rows, 128), jnp.float32)] + [bf16(3, rows, width)] * GROUP,
        compiler_params=params,
        cost_estimate=pl.CostEstimate(flops=30 * rows * local_width, bytes_accessed=22 * rows * local_width, transcendentals=0),
        name="values",
    )(places, shares, clean_qkv, noise_qkv, attended_grad)
    sums_other = other_core(sums)
    values = [values[0]] + [swap(values[d], d) for d in range(1, GROUP)]

    keys = pl.pallas_call(
        functools.partial(keys_kernel, width, sizes),
        grid=grid,
        in_specs=[smem, smem, by_rows(2, local_width), by_rows(2, local_width), gain_spec, flat(128), flat(128)],
        out_specs=[by_rows(3, heads * HEAD_DIM) for heads in sizes for _ in range(GROUP)],
        out_shape=[bf16(3, rows, heads * HEAD_DIM) for heads in sizes for _ in range(GROUP)],
        compiler_params=params,
        cost_estimate=pl.CostEstimate(flops=30 * rows * local_width, bytes_accessed=14 * rows * local_width, transcendentals=0),
        name="keys",
    )(places, shares, clean_qkv, noise_qkv, gains, sums, sums_other)

    total = lax.axis_size("tm")
    up = [(i, i + GROUP) for i in range(total - GROUP)]
    down = [(i + GROUP, i) for i in range(total - GROUP)]
    backs, ctxs = [], []
    offset = 0
    for chunk, heads in enumerate(sizes):
        count = heads * HEAD_DIM
        mine = keys[chunk * GROUP : (chunk + 1) * GROUP]
        key_parts = [mine[0]] + [swap(mine[d], d) for d in range(1, GROUP)]
        halo = jnp.stack(
            [part[0, :, offset : offset + count] for part in values] + [part[0] for part in key_parts]
        )
        halo = lax.ppermute(halo, "tm", up)
        at = offset // HEAD_DIM
        one = lambda lead, start=0: pl.BlockSpec(lead + (rows, HEAD_DIM), lambda h: (0,) * len(lead) + (0, h + start))
        *back, ctx, halo_grad = pl.pallas_call(
            attention_kernel,
            grid=(heads,),
            in_specs=[smem, smem] + [one((3,), at)] * GROUP + [one((3,))] * GROUP + [one((2 * GROUP,))],
            out_specs=[one((3,))] * GROUP + [one((GROUP, 2))] * 2,
            out_shape=[bf16(3, rows, count)] * GROUP
            + [jax.ShapeDtypeStruct((GROUP, 2, rows, count), jnp.float32), bf16(GROUP, 2, rows, count)],
            scratch_shapes=[
                pltpu.VMEM((2 * GROUP, rows, HEAD_DIM), jnp.bfloat16),
                pltpu.VMEM((2 * GROUP, rows, HEAD_DIM), jnp.bfloat16),
                pltpu.VMEM((GROUP, rows, HEAD_DIM), jnp.bfloat16),
                pltpu.VMEM((GROUP, rows, HEAD_DIM), jnp.bfloat16),
                pltpu.VMEM((GROUP, rows, HEAD_DIM), jnp.bfloat16),
                pltpu.VMEM((GROUP, rows, HEAD_DIM), jnp.bfloat16),
                pltpu.VMEM((GROUP, 3, rows, HEAD_DIM), jnp.bfloat16),
                pltpu.VMEM((2 * GROUP, rows, HEAD_DIM), jnp.float32),
                pltpu.VMEM((2 * GROUP, rows, HEAD_DIM), jnp.float32),
            ],
            compiler_params=params,
            cost_estimate=pl.CostEstimate(
                flops=heads * 2 * 12 * GROUP * (CONTEXT + 1) * rows * rows * HEAD_DIM,
                bytes_accessed=heads * 64 * rows * HEAD_DIM * 2,
                transcendentals=heads * GROUP * (CONTEXT + 1) * rows * rows,
            ),
            name="attention",
        )(places, keeps, *values, *key_parts, halo)
        backs += [back[0]] + [swap(back[d], d) for d in range(1, GROUP)]
        later = lax.ppermute(halo_grad, "tm", down)
        summed = [(ctx[d] + later[d].astype(jnp.float32)).astype(jnp.bfloat16) for d in range(GROUP)]
        ctxs += [summed[0]] + [swap(summed[d], d) for d in range(1, GROUP)]
        offset += count

    piece_specs = [by_rows(3, heads * HEAD_DIM) for heads in sizes for _ in range(GROUP)]
    ctx_specs = [by_rows(2, heads * HEAD_DIM) for heads in sizes for _ in range(GROUP)]
    attended, inner = pl.pallas_call(
        functools.partial(inner_kernel, width, sizes),
        grid=grid,
        in_specs=[smem, smem, by_rows(2, local_width), by_rows(2, local_width), gain_spec] + piece_specs + ctx_specs,
        out_specs=[flat(local_width), flat(128)],
        out_shape=[bf16(rows, local_width), jax.ShapeDtypeStruct((rows, 128), jnp.float32)],
        compiler_params=params,
        name="inner",
    )(places, shares, clean_qkv, noise_qkv, gains, *backs, *ctxs)
    inner_other = other_core(inner)
    clean_grads = pl.pallas_call(
        functools.partial(finish_kernel, width, sizes),
        grid=grid,
        in_specs=[smem, smem, by_rows(2, local_width), by_rows(2, local_width), gain_spec]
        + [flat(128)] * 4 + piece_specs + ctx_specs,
        out_specs=by_rows(3, local_width),
        out_shape=jax.ShapeDtypeStruct((3, rows, local_width), jnp.float32),
        compiler_params=params,
        name="finish",
    )(places, shares, clean_qkv, noise_qkv, gains, sums, sums_other, inner, inner_other, *backs, *ctxs)
    return (attended, clean_grads)


def solution(mesh):
    placed = (
        P(None, "tm", "head"),
        P(None, "tm", "head"),
        P("tm"),
        P("head"),
        P("head"),
        P("tm", "head"),
    )
    heads_here = D // HEAD_DIM // mesh.shape["head"]
    grouped = mesh.shape["head"] == 2 and mesh.shape["tm"] % GROUP == 0 and heads_here % GROUP == 0
    return jax.shard_map(
        on_group if grouped else on_device,
        mesh=mesh,
        in_specs=placed,
        out_specs=(P("tm", "head"), P(None, "tm", "head")),
        check_vma=False,
    )
```

```python
import functools
import jax
import jax.numpy as jnp
from jax import lax
from jax.experimental import pallas as pl
from jax.experimental.pallas import tpu as pltpu
from jax.sharding import PartitionSpec as P

D = 5120
HEAD_DIM = 128
CONTEXT = 3


epsilon = 1e-06
masked_score = -1e30


def from_behind(block, axis, distance):
    devices = range(lax.axis_size(axis))
    route = [(i - distance, i) for i in devices if i - distance in devices]
    return lax.ppermute(block, axis, route)


def noise_share_of(timestep):
    level = timestep.astype(jnp.float32) / 1000.0
    return 5.0 * level / (1.0 + 4.0 * level)


def contract(left, right, left_dim, right_dim):
    return lax.dot_general(
        left, right, (((left_dim,), (right_dim,)), ((), ())), preferred_element_type=jnp.float32
    )


def on_device(clean_qkv, noise_qkv, timestep, gain_q, gain_k, attended_grad):
    row_count = clean_qkv.shape[1]
    local_width = clean_qkv.shape[2]
    heads_here = local_width // HEAD_DIM
    span_index = lax.axis_index("tm")
    noise_share = noise_share_of(timestep[0])
    keep_share = 1.0 - noise_share
    clean_field = clean_qkv.astype(jnp.float32)
    noisy_field = keep_share * clean_field + noise_share * noise_qkv.astype(jnp.float32)
    partial_sums = jnp.stack(
        [
            jnp.sum(noisy_field[0] * noisy_field[0], axis=-1),
            jnp.sum(noisy_field[1] * noisy_field[1], axis=-1),
            jnp.sum(clean_field[1] * clean_field[1], axis=-1),
        ]
    )
    totals = lax.psum(partial_sums, "head")
    inverse = lax.rsqrt(totals / D + epsilon)
    query_rows = (noisy_field[0] * inverse[0][:, None] * gain_q).astype(jnp.bfloat16)
    key_own = (noisy_field[1] * inverse[1][:, None] * gain_k).astype(jnp.bfloat16)
    key_clean = (clean_field[1] * inverse[2][:, None] * gain_k).astype(jnp.bfloat16)
    value_own = noisy_field[2].astype(jnp.bfloat16)
    value_clean = clean_qkv[2]
    outgoing = jnp.stack([key_clean, value_clean])
    arrived = []
    for hop_index in range(CONTEXT):
        arrived.append(from_behind(outgoing, "tm", hop_index + 1))
    key_rows = jnp.concatenate([key_own] + [piece[0] for piece in arrived], axis=0)
    value_rows = jnp.concatenate([value_own] + [piece[1] for piece in arrived], axis=0)
    block_ids = jnp.arange(CONTEXT + 1, dtype=jnp.int32)
    block_valid = span_index >= block_ids
    key_valid = jnp.repeat(block_valid, row_count)
    score_scale = HEAD_DIM ** (-0.5)
    key_count = (CONTEXT + 1) * row_count

    def one_head(head_index, carried_state):
        output_acc, query_acc, keys_acc, values_acc, stat_acc = carried_state
        head_start = head_index * HEAD_DIM
        query_head = lax.dynamic_slice_in_dim(query_rows, head_start, HEAD_DIM, 1)
        key_head = lax.dynamic_slice_in_dim(key_rows, head_start, HEAD_DIM, 1)
        value_head = lax.dynamic_slice_in_dim(value_rows, head_start, HEAD_DIM, 1)
        grad_head = lax.dynamic_slice_in_dim(attended_grad, head_start, HEAD_DIM, 1)
        scores = contract(query_head, key_head, 1, 1) * score_scale
        scores = jnp.where(key_valid[None, :], scores, masked_score)
        row_max = jnp.max(scores, axis=-1, keepdims=True)
        exponent = jnp.exp(scores - row_max)
        row_total = jnp.sum(exponent, axis=-1, keepdims=True)
        attention = exponent / row_total
        weights = attention.astype(jnp.bfloat16)
        output_head = jnp.dot(weights, value_head, preferred_element_type=jnp.float32)
        grad_probs = contract(grad_head, value_head, 1, 1)
        row_delta = jnp.sum(attention * grad_probs, axis=-1, keepdims=True)
        grad_scores = (attention * (grad_probs - row_delta) * score_scale).astype(jnp.bfloat16)
        grad_query_head = jnp.dot(grad_scores, key_head, preferred_element_type=jnp.float32)
        grad_key_head = contract(grad_scores, query_head, 0, 0)
        grad_value_head = contract(weights, grad_head, 0, 0)
        head_stats = jnp.stack([row_max[:, 0], row_total[:, 0], row_delta[:, 0]])[:, None, :]
        output_acc = lax.dynamic_update_slice_in_dim(output_acc, output_head, head_start, 1)
        query_acc = lax.dynamic_update_slice_in_dim(query_acc, grad_query_head, head_start, 1)
        keys_acc = lax.dynamic_update_slice_in_dim(keys_acc, grad_key_head, head_start, 1)
        values_acc = lax.dynamic_update_slice_in_dim(values_acc, grad_value_head, head_start, 1)
        stat_acc = lax.dynamic_update_slice_in_dim(stat_acc, head_stats, head_index, 1)
        return (output_acc, query_acc, keys_acc, values_acc, stat_acc)

    start_state = (
        jnp.zeros((row_count, local_width), jnp.float32),
        jnp.zeros((row_count, local_width), jnp.float32),
        jnp.zeros((key_count, local_width), jnp.float32),
        jnp.zeros((key_count, local_width), jnp.float32),
        jnp.zeros((3, heads_here, row_count), jnp.float32),
    )
    output_acc, grad_query, grad_keys, grad_values, row_stats = lax.fori_loop(
        0, heads_here, one_head, start_state
    )
    attended = output_acc.astype(jnp.bfloat16)
    returns_parts = []
    for hop_index in range(1, CONTEXT + 1):
        lower = hop_index * row_count
        returns_parts.append(
            jnp.stack(
                [grad_keys[lower : lower + row_count], grad_values[lower : lower + row_count]]
            )
        )
    context_grads = jnp.zeros_like(returns_parts[0])
    for hop_index in range(CONTEXT):
        context_grads = context_grads + from_behind(
            returns_parts[hop_index], "tm", -(hop_index + 1)
        )
    context_key_grad = context_grads[0]
    context_value_grad = context_grads[1]
    own_key_grad = grad_keys[:row_count]
    inner_sums = jnp.stack(
        [
            jnp.sum(noisy_field[0] * gain_q * grad_query, axis=-1),
            jnp.sum(noisy_field[1] * gain_k * own_key_grad, axis=-1),
            jnp.sum(clean_field[1] * gain_k * context_key_grad, axis=-1),
        ]
    )
    inner_totals = lax.psum(inner_sums, "head")
    cube_term = inverse**3 * inner_totals / D
    grad_query_pre = (
        inverse[0][:, None] * gain_q * grad_query - noisy_field[0] * cube_term[0][:, None]
    )
    grad_own_pre = (
        inverse[1][:, None] * gain_k * own_key_grad - noisy_field[1] * cube_term[1][:, None]
    )
    grad_clean_pre = (
        inverse[2][:, None] * gain_k * context_key_grad - clean_field[1] * cube_term[2][:, None]
    )
    clean_grads = jnp.stack(
        [
            keep_share * grad_query_pre,
            keep_share * grad_own_pre + grad_clean_pre,
            keep_share * grad_values[:row_count] + context_value_grad,
        ]
    )
    return (attended, clean_grads)


GROUP = 4
ROWS = 64
LOG2E = 1.4426950408889634
VMEM_LIMIT = 48 * 1024 * 1024
EXCHANGE_VMEM = 62 * 1024 * 1024


def other_core(block):
    return lax.ppermute(block, "head", [(0, 1), (1, 0)])


def columns_at(place, width, offset, count):
    return pl.ds(pl.multiple_of(place * width + offset, HEAD_DIM), count)


def pack_lanes(parts):
    lane = lax.broadcasted_iota(jnp.int32, (parts[0].shape[0], 128), 1)
    packed = jnp.zeros((parts[0].shape[0], 128), jnp.float32)
    for index, part in enumerate(parts):
        packed = jnp.where(lane == index, part, packed)
    return packed


def sums_kernel(share_ref, clean_ref, noise_ref, sums_ref):
    keep, share = share_ref[0], share_ref[1]
    clean_key = clean_ref[1].astype(jnp.float32)
    query = keep * clean_ref[0].astype(jnp.float32) + share * noise_ref[0].astype(jnp.float32)
    key = keep * clean_key + share * noise_ref[1].astype(jnp.float32)
    sums_ref[...] = pack_lanes([jnp.sum(field * field, axis=-1, keepdims=True) for field in (query, key, clean_key)])


def pack_kernel(heads, place_ref, share_ref, clean_ref, noise_ref, grad_ref, gains_ref, sums_ref, other_ref, packed_ref):
    keep, share = share_ref[0], share_ref[1]
    place = place_ref[0]
    inverse = lax.rsqrt((sums_ref[...] + other_ref[...]) / D + epsilon)
    for distance in range(GROUP):
        for head in range(heads):
            cols = columns_at(place ^ distance, heads * HEAD_DIM, head * HEAD_DIM, HEAD_DIM)
            gain_q, gain_k = gains_ref[0:1, cols], gains_ref[1:2, cols]
            clean_value = clean_ref[2, :, cols]
            clean_key = clean_ref[1, :, cols].astype(jnp.float32)
            query = keep * clean_ref[0, :, cols].astype(jnp.float32) + share * noise_ref[0, :, cols].astype(jnp.float32)
            key = keep * clean_key + share * noise_ref[1, :, cols].astype(jnp.float32)
            value = keep * clean_value.astype(jnp.float32) + share * noise_ref[2, :, cols].astype(jnp.float32)
            packed_ref[head, distance, 0] = clean_value
            packed_ref[head, distance, 1] = (clean_key * inverse[:, 2:3] * gain_k).astype(jnp.bfloat16)
            packed_ref[head, distance, 2] = value.astype(jnp.bfloat16)
            packed_ref[head, distance, 3] = (key * inverse[:, 1:2] * gain_k).astype(jnp.bfloat16)
            packed_ref[head, distance, 4] = (query * inverse[:, 0:1] * gain_q).astype(jnp.bfloat16)
            packed_ref[head, distance, 5] = grad_ref[:, cols]


BACK_SLOTS = 3


def exchange_kernel(
    heads, layers, packed_ref, keep_ref, home_ref,
    taken, halo, halo_back, back, halo_out, keeps, keys, values, key_acc, value_acc,
    own_sem, take_send, take_recv, keep_send, keep_recv, up_send, up_recv, down_send, down_recv,
    own_back_sem, back_send, back_recv, own_ctx_sem, ctx_send, ctx_recv,
):
    tm = lax.axis_index("tm")
    total = layers * GROUP
    layer, place = lax.div(tm, GROUP), lax.rem(tm, GROUP)
    low, high = lax.rem(place, 2), lax.div(place, 2)
    not_first = lax.div(layer + layers - 1, layers)
    not_last = lax.div(2 * layers - 2 - layer, layers)
    scale = HEAD_DIM ** (-0.5)

    def across(spot):
        return lax.rem(lax.rem(spot, 2) + low, 2) + 2 * lax.rem(lax.div(spot, 2) + high, 2)

    def partner(distance):
        return {"tm": layer * GROUP + across(jnp.int32(distance))}

    def remote(src, dst, send, recv, target):
        return pltpu.make_async_remote_copy(
            src_ref=src, dst_ref=dst, send_sem=send, recv_sem=recv,
            device_id=target, device_id_type=pl.DeviceIdType.MESH,
        )

    def own(head):
        return pltpu.make_async_copy(packed_ref.at[head, 0], taken.at[head, 0], own_sem.at[head])

    def take(head, d):
        return remote(
            packed_ref.at[head, d], taken.at[head, d], take_send.at[head, d], take_recv.at[head, d], partner(d)
        )

    def keep_copy(d):
        return remote(keep_ref, keeps.at[d], keep_send.at[d], keep_recv.at[d], partner(d))

    def up(head):
        return remote(
            taken.at[head, :, pl.ds(0, 2)], halo.at[head], up_send.at[head], up_recv.at[head], {"tm": lax.rem(tm + GROUP, total)}
        )

    def down(head):
        return remote(
            halo_out.at[lax.rem(head, 2)], halo_back.at[head], down_send.at[head], down_recv.at[head], {"tm": lax.rem(tm + total - GROUP, total)}
        )

    def own_back(head):
        return pltpu.make_async_copy(
            back.at[lax.rem(head, BACK_SLOTS), 0, pl.ds(0, 3)], home_ref.at[head, 0, pl.ds(0, 3)], own_back_sem.at[head]
        )

    def give(head, d):
        return remote(
            back.at[lax.rem(head, BACK_SLOTS), d, pl.ds(0, 3)], home_ref.at[head, d, pl.ds(0, 3)],
            back_send.at[head, d], back_recv.at[head, d], partner(d),
        )

    def own_ctx(head):
        return pltpu.make_async_copy(
            back.at[lax.rem(head, BACK_SLOTS), 0, pl.ds(3, 2)], home_ref.at[head, 0, pl.ds(3, 2)], own_ctx_sem.at[head]
        )

    def give_ctx(head, d):
        return remote(
            back.at[lax.rem(head, BACK_SLOTS), d, pl.ds(3, 2)], home_ref.at[head, d, pl.ds(3, 2)],
            ctx_send.at[head, d], ctx_recv.at[head, d], partner(d),
        )

    def start_take(head):
        own(head).start()
        for d in range(1, GROUP):
            take(head, d).start()

    def drain_sends(head):
        own_back(head).wait()
        own_ctx(head).wait()
        for d in range(1, GROUP):
            give(head, d).wait_send()
            give_ctx(head, d).wait_send()

    barrier = pltpu.get_barrier_semaphore()
    for d in range(1, GROUP):
        pl.semaphore_signal(barrier, inc=1, device_id=partner(d), device_id_type=pl.DeviceIdType.MESH)

    @pl.when(not_first == 1)
    def _():
        pl.semaphore_signal(barrier, inc=1, device_id={"tm": tm - GROUP}, device_id_type=pl.DeviceIdType.MESH)

    @pl.when(not_last == 1)
    def _():
        pl.semaphore_signal(barrier, inc=1, device_id={"tm": tm + GROUP}, device_id_type=pl.DeviceIdType.MESH)

    pl.semaphore_wait(barrier, GROUP - 1 + not_first + not_last)

    for d in range(1, GROUP):
        keep_copy(d).start()
    for head in range(min(2, heads)):
        start_take(jnp.int32(head))
    keeps[0] = keep_ref[...]
    for d in range(1, GROUP):
        keep_copy(d).wait_recv()

    def attention(head):
        parity = lax.rem(head, 2)
        slot_back = lax.rem(head, BACK_SLOTS)
        for distance in range(GROUP):
            spot = across(jnp.int32(distance))
            values[spot] = halo[head, distance, 0]
            keys[spot] = halo[head, distance, 1]
            values[GROUP + spot] = taken[head, distance, 0]
            keys[GROUP + spot] = taken[head, distance, 1]
        key_acc[parity] = jnp.zeros(key_acc.shape[1:], jnp.float32)
        value_acc[parity] = jnp.zeros(value_acc.shape[1:], jnp.float32)

        def one_span(span, carry):
            d = across(span)
            query, grad = taken[head, d, 4], taken[head, d, 5]
            slots = [span + GROUP - hop for hop in range(1, CONTEXT + 1)]
            key_blocks = [taken[head, d, 3]] + [keys[slot] for slot in slots]
            value_blocks = [taken[head, d, 2]] + [values[slot] for slot in slots]
            absent = [0.0] + [
                jnp.where(jnp.logical_and(not_first == 0, slot < GROUP), -masked_score, 0.0) for slot in slots
            ]
            scores = [contract(block, query, 1, 1) * (scale * LOG2E) for block in key_blocks]
            top = functools.reduce(
                jnp.maximum,
                [jnp.max(part, axis=0, keepdims=True) - lack for part, lack in zip(scores, absent)],
            )
            exponents = [jnp.exp2(part - (top + lack)) for part, lack in zip(scores, absent)]
            total = sum(jnp.sum(part, axis=0, keepdims=True) for part in exponents)
            recip = 1.0 / total
            attention = [part * recip for part in exponents]
            weights = [part.astype(jnp.bfloat16) for part in attention]
            output = sum(contract(block, part, 0, 0) for block, part in zip(value_blocks, weights))
            grad_turned = jnp.transpose(grad.astype(jnp.float32))
            delta = jnp.sum(output * grad_turned, axis=0, keepdims=True)
            back[slot_back, d, 0] = jnp.transpose(output).astype(jnp.bfloat16)
            grad_query = 0.0
            for index in range(CONTEXT + 1):
                probs = contract(value_blocks[index], grad, 1, 1)
                change = (attention[index] * (probs - delta) * scale).astype(jnp.bfloat16)
                grad_query = grad_query + contract(key_blocks[index], change, 0, 0)
                grad_key = jnp.dot(change, query, preferred_element_type=jnp.float32)
                grad_value = jnp.dot(weights[index], grad, preferred_element_type=jnp.float32)
                if index == 0:
                    back[slot_back, d, 2] = grad_key.astype(jnp.bfloat16)
                    own_slot = GROUP + span
                    value_acc[parity, own_slot] = value_acc[parity, own_slot] + keeps[d, 0:1] * grad_value
                else:
                    slot = slots[index - 1]
                    key_acc[parity, slot] = key_acc[parity, slot] + grad_key
                    value_acc[parity, slot] = value_acc[parity, slot] + grad_value
            back[slot_back, d, 1] = jnp.transpose(grad_query).astype(jnp.bfloat16)
            return carry

        lax.fori_loop(0, GROUP, one_span, 0)
        for distance in range(GROUP):
            spot = across(jnp.int32(distance))
            halo_out[parity, distance, 0] = value_acc[parity, spot].astype(jnp.bfloat16)
            halo_out[parity, distance, 1] = key_acc[parity, spot].astype(jnp.bfloat16)

    def step(index, carry):
        @pl.when(index < heads)
        def _():
            own(index).wait()
            for d in range(1, GROUP):
                take(index, d).wait_recv()

            @pl.when(not_last == 1)
            def _():
                up(index).start()

            @pl.when(index + 2 < heads)
            def _():
                start_take(index + 2)

            @pl.when(not_first == 0)
            def _():
                halo[index] = jnp.zeros(halo.shape[1:], halo.dtype)

        @pl.when(jnp.logical_and(index >= 1, index <= heads))
        def _():
            head = index - 1

            @pl.when(not_first == 1)
            def _():
                up(head).wait_recv()

            @pl.when(head >= BACK_SLOTS)
            def _():
                drain_sends(head - BACK_SLOTS)

            @pl.when(jnp.logical_and(head >= 2, not_first == 1))
            def _():
                down(head - 2).wait_send()

            attention(head)
            own_back(head).start()
            for d in range(1, GROUP):
                give(head, d).start()

            @pl.when(not_first == 1)
            def _():
                down(head).start()

        @pl.when(index >= 2)
        def _():
            head = index - 2
            parity = lax.rem(head, 2)
            slot_back = lax.rem(head, BACK_SLOTS)

            @pl.when(not_last == 1)
            def _():
                down(head).wait_recv()

            @pl.when(not_last == 0)
            def _():
                halo_back[head] = jnp.zeros(halo_back.shape[1:], halo_back.dtype)

            for distance in range(GROUP):
                spot = GROUP + across(jnp.int32(distance))
                grad_key = key_acc[parity, spot] + halo_back[head, distance, 1].astype(jnp.float32)
                grad_value = value_acc[parity, spot] + halo_back[head, distance, 0].astype(jnp.float32)
                back[slot_back, distance, 3] = grad_key.astype(jnp.bfloat16)
                back[slot_back, distance, 4] = grad_value.astype(jnp.bfloat16)
            own_ctx(head).start()
            for d in range(1, GROUP):
                give_ctx(head, d).start()

        return carry

    lax.fori_loop(0, heads + 2, step, 0)

    def finish_head(head, carry):
        for d in range(1, GROUP):
            take(head, d).wait_send()
            give(head, d).wait_recv()
            give_ctx(head, d).wait_recv()

        @pl.when(not_last == 1)
        def _():
            up(head).wait_send()

        @pl.when(head >= heads - BACK_SLOTS)
        def _():
            drain_sends(head)

        @pl.when(jnp.logical_and(head >= heads - 2, not_first == 1))
        def _():
            down(head).wait_send()

        return carry

    lax.fori_loop(0, heads, finish_head, 0)
    for d in range(1, GROUP):
        keep_copy(d).wait_send()


def noisy_at(clean_ref, noise_ref, index, cols, keep, share):
    return keep * clean_ref[index, :, cols].astype(jnp.float32) + share * noise_ref[index, :, cols].astype(jnp.float32)


def inner_kernel(heads, place_ref, share_ref, clean_ref, noise_ref, gains_ref, home_ref, inner_ref):
    keep, share = share_ref[0], share_ref[1]
    place = place_ref[0]
    inner = [0.0, 0.0, 0.0]
    for distance in range(GROUP):
        for head in range(heads):
            cols = columns_at(place ^ distance, heads * HEAD_DIM, head * HEAD_DIM, HEAD_DIM)
            gain_q, gain_k = gains_ref[0:1, cols], gains_ref[1:2, cols]
            terms = (
                noisy_at(clean_ref, noise_ref, 0, cols, keep, share) * gain_q * home_ref[head, distance, 1].astype(jnp.float32),
                noisy_at(clean_ref, noise_ref, 1, cols, keep, share) * gain_k * home_ref[head, distance, 2].astype(jnp.float32),
                clean_ref[1, :, cols].astype(jnp.float32) * gain_k * home_ref[head, distance, 3].astype(jnp.float32),
            )
            for index, term in enumerate(terms):
                inner[index] = inner[index] + term
    inner_ref[...] = pack_lanes([jnp.sum(part, axis=-1, keepdims=True) for part in inner])


def finish_kernel(
    heads, place_ref, share_ref, clean_ref, noise_ref, gains_ref,
    sums_ref, sums_other_ref, inner_ref, inner_other_ref, home_ref, attended_ref, grads_ref
):
    keep, share = share_ref[0], share_ref[1]
    place = place_ref[0]
    inverse = lax.rsqrt((sums_ref[...] + sums_other_ref[...]) / D + epsilon)
    cube = inverse * inverse * inverse * ((inner_ref[...] + inner_other_ref[...]) / D)
    for distance in range(GROUP):
        for head in range(heads):
            cols = columns_at(place ^ distance, heads * HEAD_DIM, head * HEAD_DIM, HEAD_DIM)
            gain_q, gain_k = gains_ref[0:1, cols], gains_ref[1:2, cols]
            query = noisy_at(clean_ref, noise_ref, 0, cols, keep, share)
            key = noisy_at(clean_ref, noise_ref, 1, cols, keep, share)
            clean_key = clean_ref[1, :, cols].astype(jnp.float32)
            grad = [home_ref[head, distance, which].astype(jnp.float32) for which in range(1, 5)]
            grad_query = inverse[:, 0:1] * gain_q * grad[0] - query * cube[:, 0:1]
            grad_own = inverse[:, 1:2] * gain_k * grad[1] - key * cube[:, 1:2]
            grad_clean = inverse[:, 2:3] * gain_k * grad[2] - clean_key * cube[:, 2:3]
            attended_ref[:, cols] = home_ref[head, distance, 0]
            grads_ref[0, :, cols] = keep * grad_query
            grads_ref[1, :, cols] = keep * grad_own + grad_clean
            grads_ref[2, :, cols] = grad[3]


def on_group(clean_qkv, noise_qkv, timestep, gain_q, gain_k, attended_grad):
    rows, local_width = clean_qkv.shape[1:]
    heads = local_width // GROUP // HEAD_DIM
    layers = lax.axis_size("tm") // GROUP
    places = lax.rem(lax.axis_index("tm"), GROUP).astype(jnp.int32)[None]
    noise_share = noise_share_of(timestep[0])
    keep_share = 1.0 - noise_share
    shares = jnp.stack([keep_share, noise_share])
    gains = jnp.stack([gain_q, gain_k])
    keep_tile = jnp.full((8, 128), keep_share, jnp.float32)

    smem = pl.BlockSpec(memory_space=pltpu.SMEM)
    params = pltpu.CompilerParams(vmem_limit_bytes=VMEM_LIMIT)
    grid = (rows // ROWS,)
    by_rows = lambda parts: pl.BlockSpec((parts, ROWS, local_width), lambda i: (0, i, 0))
    flat = lambda count: pl.BlockSpec((ROWS, count), lambda i: (i, 0))
    by_head = lambda parts: pl.BlockSpec((heads, GROUP, parts, ROWS, HEAD_DIM), lambda i: (0, 0, 0, i, 0))
    gain_spec = pl.BlockSpec((2, local_width), lambda i: (0, 0))
    lanes = jax.ShapeDtypeStruct((rows, 128), jnp.float32)

    sums = pl.pallas_call(
        sums_kernel,
        grid=grid,
        in_specs=[smem, by_rows(2), by_rows(2)],
        out_specs=flat(128),
        out_shape=lanes,
        compiler_params=params,
        name="sums",
    )(shares, clean_qkv, noise_qkv)
    sums_other = other_core(sums)
    packed = pl.pallas_call(
        functools.partial(pack_kernel, heads),
        grid=grid,
        in_specs=[smem, smem, by_rows(3), by_rows(3), flat(local_width), gain_spec, flat(128), flat(128)],
        out_specs=by_head(6),
        out_shape=jax.ShapeDtypeStruct((heads, GROUP, 6, rows, HEAD_DIM), jnp.bfloat16),
        compiler_params=params,
        name="pack",
    )(places, shares, clean_qkv, noise_qkv, attended_grad, gains, sums, sums_other)

    half = lambda *lead: pltpu.VMEM(lead + (rows, HEAD_DIM), jnp.bfloat16)
    full = lambda *lead: pltpu.VMEM(lead + (rows, HEAD_DIM), jnp.float32)
    copies = lambda *shape: pltpu.SemaphoreType.DMA(shape)
    home = pl.pallas_call(
        functools.partial(exchange_kernel, heads, layers),
        in_specs=[pl.BlockSpec(memory_space=pl.ANY), pl.BlockSpec(memory_space=pltpu.VMEM)],
        out_specs=pl.BlockSpec(memory_space=pl.ANY),
        out_shape=jax.ShapeDtypeStruct((heads, GROUP, 5, rows, HEAD_DIM), jnp.bfloat16),
        scratch_shapes=[
            half(heads, GROUP, 6),
            half(heads, GROUP, 2),
            half(heads, GROUP, 2),
            half(BACK_SLOTS, GROUP, 5),
            half(2, GROUP, 2),
            pltpu.VMEM((GROUP, 8, 128), jnp.float32),
            half(2 * GROUP),
            half(2 * GROUP),
            full(2, 2 * GROUP),
            full(2, 2 * GROUP),
            copies(heads),
            copies(heads, GROUP), copies(heads, GROUP),
            copies(GROUP), copies(GROUP),
            copies(heads), copies(heads),
            copies(heads), copies(heads),
            copies(heads),
            copies(heads, GROUP), copies(heads, GROUP),
            copies(heads),
            copies(heads, GROUP), copies(heads, GROUP),
        ],
        compiler_params=pltpu.CompilerParams(
            vmem_limit_bytes=EXCHANGE_VMEM, collective_id=0, has_side_effects=True
        ),
        cost_estimate=pl.CostEstimate(
            flops=heads * 2 * 6 * GROUP * (CONTEXT + 1) * rows * rows * HEAD_DIM,
            bytes_accessed=heads * GROUP * 22 * rows * HEAD_DIM,
            transcendentals=heads * GROUP * (CONTEXT + 1) * rows * rows,
        ),
        name="exchange",
    )(packed, keep_tile)

    inner = pl.pallas_call(
        functools.partial(inner_kernel, heads),
        grid=grid,
        in_specs=[smem, smem, by_rows(2), by_rows(2), gain_spec, by_head(5)],
        out_specs=flat(128),
        out_shape=lanes,
        compiler_params=params,
        name="inner",
    )(places, shares, clean_qkv, noise_qkv, gains, home)
    inner_other = other_core(inner)
    attended, clean_grads = pl.pallas_call(
        functools.partial(finish_kernel, heads),
        grid=grid,
        in_specs=[smem, smem, by_rows(2), by_rows(2), gain_spec] + [flat(128)] * 4 + [by_head(5)],
        out_specs=[flat(local_width), by_rows(3)],
        out_shape=[
            jax.ShapeDtypeStruct((rows, local_width), jnp.bfloat16),
            jax.ShapeDtypeStruct((3, rows, local_width), jnp.float32),
        ],
        compiler_params=params,
        name="finish",
    )(places, shares, clean_qkv, noise_qkv, gains, sums, sums_other, inner, inner_other, home)
    return (attended, clean_grads)


def solution(mesh):
    placed = (
        P(None, "tm", "head"),
        P(None, "tm", "head"),
        P("tm"),
        P("head"),
        P("head"),
        P("tm", "head"),
    )
    heads_here = D // HEAD_DIM // mesh.shape["head"]
    grouped = mesh.shape["head"] == 2 and mesh.shape["tm"] % GROUP == 0 and heads_here % GROUP == 0
    return jax.shard_map(
        on_group if grouped else on_device,
        mesh=mesh,
        in_specs=placed,
        out_specs=(P("tm", "head"), P(None, "tm", "head")),
        check_vma=False,
    )
```

```python
import functools
import jax
import jax.numpy as jnp
from jax import lax
from jax.experimental import pallas as pl
from jax.experimental.pallas import tpu as pltpu
from jax.sharding import PartitionSpec as P

D = 5120
HEAD_DIM = 128
CONTEXT = 3


epsilon = 1e-06
masked_score = -1e30


def from_behind(block, axis, distance):
    devices = range(lax.axis_size(axis))
    route = [(i - distance, i) for i in devices if i - distance in devices]
    return lax.ppermute(block, axis, route)


def noise_share_of(timestep):
    level = timestep.astype(jnp.float32) / 1000.0
    return 5.0 * level / (1.0 + 4.0 * level)


def contract(left, right, left_dim, right_dim):
    return lax.dot_general(
        left, right, (((left_dim,), (right_dim,)), ((), ())), preferred_element_type=jnp.float32
    )


def on_device(clean_qkv, noise_qkv, timestep, gain_q, gain_k, attended_grad):
    row_count = clean_qkv.shape[1]
    local_width = clean_qkv.shape[2]
    heads_here = local_width // HEAD_DIM
    span_index = lax.axis_index("tm")
    noise_share = noise_share_of(timestep[0])
    keep_share = 1.0 - noise_share
    clean_field = clean_qkv.astype(jnp.float32)
    noisy_field = keep_share * clean_field + noise_share * noise_qkv.astype(jnp.float32)
    partial_sums = jnp.stack(
        [
            jnp.sum(noisy_field[0] * noisy_field[0], axis=-1),
            jnp.sum(noisy_field[1] * noisy_field[1], axis=-1),
            jnp.sum(clean_field[1] * clean_field[1], axis=-1),
        ]
    )
    totals = lax.psum(partial_sums, "head")
    inverse = lax.rsqrt(totals / D + epsilon)
    query_rows = (noisy_field[0] * inverse[0][:, None] * gain_q).astype(jnp.bfloat16)
    key_own = (noisy_field[1] * inverse[1][:, None] * gain_k).astype(jnp.bfloat16)
    key_clean = (clean_field[1] * inverse[2][:, None] * gain_k).astype(jnp.bfloat16)
    value_own = noisy_field[2].astype(jnp.bfloat16)
    value_clean = clean_qkv[2]
    outgoing = jnp.stack([key_clean, value_clean])
    arrived = []
    for hop_index in range(CONTEXT):
        arrived.append(from_behind(outgoing, "tm", hop_index + 1))
    key_rows = jnp.concatenate([key_own] + [piece[0] for piece in arrived], axis=0)
    value_rows = jnp.concatenate([value_own] + [piece[1] for piece in arrived], axis=0)
    block_ids = jnp.arange(CONTEXT + 1, dtype=jnp.int32)
    block_valid = span_index >= block_ids
    key_valid = jnp.repeat(block_valid, row_count)
    score_scale = HEAD_DIM ** (-0.5)
    key_count = (CONTEXT + 1) * row_count

    def one_head(head_index, carried_state):
        output_acc, query_acc, keys_acc, values_acc, stat_acc = carried_state
        head_start = head_index * HEAD_DIM
        query_head = lax.dynamic_slice_in_dim(query_rows, head_start, HEAD_DIM, 1)
        key_head = lax.dynamic_slice_in_dim(key_rows, head_start, HEAD_DIM, 1)
        value_head = lax.dynamic_slice_in_dim(value_rows, head_start, HEAD_DIM, 1)
        grad_head = lax.dynamic_slice_in_dim(attended_grad, head_start, HEAD_DIM, 1)
        scores = contract(query_head, key_head, 1, 1) * score_scale
        scores = jnp.where(key_valid[None, :], scores, masked_score)
        row_max = jnp.max(scores, axis=-1, keepdims=True)
        exponent = jnp.exp(scores - row_max)
        row_total = jnp.sum(exponent, axis=-1, keepdims=True)
        attention = exponent / row_total
        weights = attention.astype(jnp.bfloat16)
        output_head = jnp.dot(weights, value_head, preferred_element_type=jnp.float32)
        grad_probs = contract(grad_head, value_head, 1, 1)
        row_delta = jnp.sum(attention * grad_probs, axis=-1, keepdims=True)
        grad_scores = (attention * (grad_probs - row_delta) * score_scale).astype(jnp.bfloat16)
        grad_query_head = jnp.dot(grad_scores, key_head, preferred_element_type=jnp.float32)
        grad_key_head = contract(grad_scores, query_head, 0, 0)
        grad_value_head = contract(weights, grad_head, 0, 0)
        head_stats = jnp.stack([row_max[:, 0], row_total[:, 0], row_delta[:, 0]])[:, None, :]
        output_acc = lax.dynamic_update_slice_in_dim(output_acc, output_head, head_start, 1)
        query_acc = lax.dynamic_update_slice_in_dim(query_acc, grad_query_head, head_start, 1)
        keys_acc = lax.dynamic_update_slice_in_dim(keys_acc, grad_key_head, head_start, 1)
        values_acc = lax.dynamic_update_slice_in_dim(values_acc, grad_value_head, head_start, 1)
        stat_acc = lax.dynamic_update_slice_in_dim(stat_acc, head_stats, head_index, 1)
        return (output_acc, query_acc, keys_acc, values_acc, stat_acc)

    start_state = (
        jnp.zeros((row_count, local_width), jnp.float32),
        jnp.zeros((row_count, local_width), jnp.float32),
        jnp.zeros((key_count, local_width), jnp.float32),
        jnp.zeros((key_count, local_width), jnp.float32),
        jnp.zeros((3, heads_here, row_count), jnp.float32),
    )
    output_acc, grad_query, grad_keys, grad_values, row_stats = lax.fori_loop(
        0, heads_here, one_head, start_state
    )
    attended = output_acc.astype(jnp.bfloat16)
    returns_parts = []
    for hop_index in range(1, CONTEXT + 1):
        lower = hop_index * row_count
        returns_parts.append(
            jnp.stack(
                [grad_keys[lower : lower + row_count], grad_values[lower : lower + row_count]]
            )
        )
    context_grads = jnp.zeros_like(returns_parts[0])
    for hop_index in range(CONTEXT):
        context_grads = context_grads + from_behind(
            returns_parts[hop_index], "tm", -(hop_index + 1)
        )
    context_key_grad = context_grads[0]
    context_value_grad = context_grads[1]
    own_key_grad = grad_keys[:row_count]
    inner_sums = jnp.stack(
        [
            jnp.sum(noisy_field[0] * gain_q * grad_query, axis=-1),
            jnp.sum(noisy_field[1] * gain_k * own_key_grad, axis=-1),
            jnp.sum(clean_field[1] * gain_k * context_key_grad, axis=-1),
        ]
    )
    inner_totals = lax.psum(inner_sums, "head")
    cube_term = inverse**3 * inner_totals / D
    grad_query_pre = (
        inverse[0][:, None] * gain_q * grad_query - noisy_field[0] * cube_term[0][:, None]
    )
    grad_own_pre = (
        inverse[1][:, None] * gain_k * own_key_grad - noisy_field[1] * cube_term[1][:, None]
    )
    grad_clean_pre = (
        inverse[2][:, None] * gain_k * context_key_grad - clean_field[1] * cube_term[2][:, None]
    )
    clean_grads = jnp.stack(
        [
            keep_share * grad_query_pre,
            keep_share * grad_own_pre + grad_clean_pre,
            keep_share * grad_values[:row_count] + context_value_grad,
        ]
    )
    return (attended, clean_grads)


GROUP = 4
ROWS = 64
LOG2E = 1.4426950408889634
VMEM_LIMIT = 48 * 1024 * 1024
EXCHANGE_VMEM = 62 * 1024 * 1024


def other_core(block):
    return lax.ppermute(block, "head", [(0, 1), (1, 0)])


def columns_at(place, width, offset, count):
    return pl.ds(pl.multiple_of(place * width + offset, HEAD_DIM), count)


def pack_lanes(parts):
    lane = lax.broadcasted_iota(jnp.int32, (parts[0].shape[0], 128), 1)
    packed = jnp.zeros((parts[0].shape[0], 128), jnp.float32)
    for index, part in enumerate(parts):
        packed = jnp.where(lane == index, part, packed)
    return packed


def spread_lanes(packed):
    return [jnp.broadcast_to(packed[:, index : index + 1], packed.shape) for index in range(3)]


def sums_kernel(share_ref, clean_ref, noise_ref, sums_ref):
    keep, share = share_ref[0], share_ref[1]
    clean_key = clean_ref[1].astype(jnp.float32)
    query = keep * clean_ref[0].astype(jnp.float32) + share * noise_ref[0].astype(jnp.float32)
    key = keep * clean_key + share * noise_ref[1].astype(jnp.float32)
    sums_ref[...] = pack_lanes([jnp.sum(field * field, axis=-1, keepdims=True) for field in (query, key, clean_key)])


def pack_kernel(heads, place_ref, share_ref, clean_ref, noise_ref, grad_ref, gains_ref, sums_ref, other_ref, packed_ref, stats_ref):
    keep, share = share_ref[0], share_ref[1]
    place = place_ref[0]
    inverse = lax.rsqrt((sums_ref[...] + other_ref[...]) / D + epsilon)
    stats_ref[...] = pack_lanes([keep * inverse[:, 1:2], inverse[:, 2:3], keep])
    inverse_q, inverse_k, inverse_clean = spread_lanes(inverse)
    for distance in range(GROUP):
        for head in range(heads):
            cols = columns_at(place ^ distance, heads * HEAD_DIM, head * HEAD_DIM, HEAD_DIM)
            gain_q, gain_k = gains_ref[0:1, cols], gains_ref[1:2, cols]
            clean_value = clean_ref[2, :, cols]
            clean_key = clean_ref[1, :, cols].astype(jnp.float32)
            query = keep * clean_ref[0, :, cols].astype(jnp.float32) + share * noise_ref[0, :, cols].astype(jnp.float32)
            key = keep * clean_key + share * noise_ref[1, :, cols].astype(jnp.float32)
            value = keep * clean_value.astype(jnp.float32) + share * noise_ref[2, :, cols].astype(jnp.float32)
            packed_ref[head, distance, 0] = clean_value
            packed_ref[head, distance, 1] = (clean_key * inverse_clean * gain_k).astype(jnp.bfloat16)
            packed_ref[head, distance, 2] = value.astype(jnp.bfloat16)
            packed_ref[head, distance, 3] = (key * inverse_k * gain_k).astype(jnp.bfloat16)
            packed_ref[head, distance, 4] = (query * inverse_q * gain_q).astype(jnp.bfloat16)
            packed_ref[head, distance, 5] = grad_ref[:, cols]


BACK_SLOTS = 3


def exchange_kernel(
    heads, layers, packed_ref, stats_ref, home_ref, inner_ref,
    taken, halo, halo_back, back, halo_out, stats, keys, values, key_acc, value_acc, own_acc, inner, inner_taken,
    own_sem, take_send, take_recv, stats_send, stats_recv, inner_send, inner_recv, up_send, up_recv, down_send, down_recv,
    own_back_sem, back_send, back_recv, own_ctx_sem, ctx_send, ctx_recv,
):
    tm = lax.axis_index("tm")
    total = layers * GROUP
    layer, place = lax.div(tm, GROUP), lax.rem(tm, GROUP)
    low, high = lax.rem(place, 2), lax.div(place, 2)
    not_first = lax.div(layer + layers - 1, layers)
    not_last = lax.div(2 * layers - 2 - layer, layers)
    scale = HEAD_DIM ** (-0.5)

    def across(spot):
        return lax.rem(lax.rem(spot, 2) + low, 2) + 2 * lax.rem(lax.div(spot, 2) + high, 2)

    def partner(distance):
        return {"tm": layer * GROUP + across(jnp.int32(distance))}

    def remote(src, dst, send, recv, target):
        return pltpu.make_async_remote_copy(
            src_ref=src, dst_ref=dst, send_sem=send, recv_sem=recv,
            device_id=target, device_id_type=pl.DeviceIdType.MESH,
        )

    def own(head):
        return pltpu.make_async_copy(packed_ref.at[head, 0], taken.at[head, 0], own_sem.at[head])

    def take(head, d):
        return remote(
            packed_ref.at[head, d], taken.at[head, d], take_send.at[head, d], take_recv.at[head, d], partner(d)
        )

    def stats_copy(d):
        return remote(stats_ref, stats.at[d], stats_send.at[d], stats_recv.at[d], partner(d))

    def inner_copy(d):
        return remote(inner.at[d], inner_taken.at[d], inner_send.at[d], inner_recv.at[d], partner(d))

    def up(head):
        return remote(
            taken.at[head, :, pl.ds(0, 2)], halo.at[head], up_send.at[head], up_recv.at[head], {"tm": lax.rem(tm + GROUP, total)}
        )

    def down(head):
        return remote(
            halo_out.at[lax.rem(head, 2)], halo_back.at[head], down_send.at[head], down_recv.at[head], {"tm": lax.rem(tm + total - GROUP, total)}
        )

    def own_back(head):
        return pltpu.make_async_copy(
            back.at[lax.rem(head, BACK_SLOTS), 0, pl.ds(0, 2)], home_ref.at[head, 0, pl.ds(0, 2)], own_back_sem.at[head]
        )

    def give(head, d):
        return remote(
            back.at[lax.rem(head, BACK_SLOTS), d, pl.ds(0, 2)], home_ref.at[head, d, pl.ds(0, 2)],
            back_send.at[head, d], back_recv.at[head, d], partner(d),
        )

    def own_ctx(head):
        return pltpu.make_async_copy(
            back.at[lax.rem(head, BACK_SLOTS), 0, pl.ds(2, 2)], home_ref.at[head, 0, pl.ds(2, 2)], own_ctx_sem.at[head]
        )

    def give_ctx(head, d):
        return remote(
            back.at[lax.rem(head, BACK_SLOTS), d, pl.ds(2, 2)], home_ref.at[head, d, pl.ds(2, 2)],
            ctx_send.at[head, d], ctx_recv.at[head, d], partner(d),
        )

    def start_take(head):
        own(head).start()
        for d in range(1, GROUP):
            take(head, d).start()

    def drain_sends(head):
        own_back(head).wait()
        own_ctx(head).wait()
        for d in range(1, GROUP):
            give(head, d).wait_send()
            give_ctx(head, d).wait_send()

    barrier = pltpu.get_barrier_semaphore()
    for d in range(1, GROUP):
        pl.semaphore_signal(barrier, inc=1, device_id=partner(d), device_id_type=pl.DeviceIdType.MESH)

    @pl.when(not_first == 1)
    def _():
        pl.semaphore_signal(barrier, inc=1, device_id={"tm": tm - GROUP}, device_id_type=pl.DeviceIdType.MESH)

    @pl.when(not_last == 1)
    def _():
        pl.semaphore_signal(barrier, inc=1, device_id={"tm": tm + GROUP}, device_id_type=pl.DeviceIdType.MESH)

    pl.semaphore_wait(barrier, GROUP - 1 + not_first + not_last)

    start_take(jnp.int32(0))
    for d in range(1, GROUP):
        stats_copy(d).start()
    if heads > 1:
        start_take(jnp.int32(1))
    stats[0] = stats_ref[...]
    inner[...] = jnp.zeros_like(inner)
    for d in range(1, GROUP):
        stats_copy(d).wait_recv()
    lane = lax.broadcasted_iota(jnp.int32, stats.shape[1:], 1)

    def add_inner(d, which, product):
        inner[d] = inner[d] + jnp.where(lane == which, jnp.sum(product, axis=-1, keepdims=True), 0.0)

    def attention(head):
        parity = lax.rem(head, 2)
        slot_back = lax.rem(head, BACK_SLOTS)
        for distance in range(GROUP):
            spot = across(jnp.int32(distance))
            values[spot] = halo[head, distance, 0]
            keys[spot] = halo[head, distance, 1]
            values[GROUP + spot] = taken[head, distance, 0]
            keys[GROUP + spot] = taken[head, distance, 1]
        key_acc[parity] = jnp.zeros(key_acc.shape[1:], jnp.float32)
        value_acc[parity] = jnp.zeros(value_acc.shape[1:], jnp.float32)

        def one_span(span, carry):
            d = across(span)
            query, grad = taken[head, d, 4], taken[head, d, 5]
            slots = [span + GROUP - hop for hop in range(1, CONTEXT + 1)]
            key_blocks = [taken[head, d, 3]] + [keys[slot] for slot in slots]
            value_blocks = [taken[head, d, 2]] + [values[slot] for slot in slots]
            absent = [0.0] + [
                jnp.where(jnp.logical_and(not_first == 0, slot < GROUP), -masked_score, 0.0) for slot in slots
            ]
            scores = [contract(block, query, 1, 1) * (scale * LOG2E) for block in key_blocks]
            top = functools.reduce(
                jnp.maximum,
                [jnp.max(part, axis=0, keepdims=True) - lack for part, lack in zip(scores, absent)],
            )
            exponents = [jnp.exp2(part - (top + lack)) for part, lack in zip(scores, absent)]
            total = sum(jnp.sum(part, axis=0, keepdims=True) for part in exponents)
            recip = 1.0 / total
            attention = [part * recip for part in exponents]
            weights = [part.astype(jnp.bfloat16) for part in attention]
            output = sum(contract(block, part, 0, 0) for block, part in zip(value_blocks, weights))
            grad_turned = jnp.transpose(grad.astype(jnp.float32))
            delta = jnp.sum(output * grad_turned, axis=0, keepdims=True)
            back[slot_back, d, 0] = jnp.transpose(output).astype(jnp.bfloat16)
            known = stats[d]
            grad_query = 0.0
            for index in range(CONTEXT + 1):
                probs = contract(value_blocks[index], grad, 1, 1)
                change = (attention[index] * (probs - delta) * scale).astype(jnp.bfloat16)
                grad_query = grad_query + contract(key_blocks[index], change, 0, 0)
                grad_key = jnp.dot(change, query, preferred_element_type=jnp.float32)
                grad_value = jnp.dot(weights[index], grad, preferred_element_type=jnp.float32)
                if index == 0:
                    add_inner(d, 1, grad_key * key_blocks[0].astype(jnp.float32))
                    own_acc[span] = known[:, 0:1] * grad_key
                    own_slot = GROUP + span
                    value_acc[parity, own_slot] = value_acc[parity, own_slot] + known[:, 2:3] * grad_value
                else:
                    slot = slots[index - 1]
                    key_acc[parity, slot] = key_acc[parity, slot] + grad_key
                    value_acc[parity, slot] = value_acc[parity, slot] + grad_value
            grad_query = jnp.transpose(grad_query)
            add_inner(d, 0, grad_query * query.astype(jnp.float32))
            back[slot_back, d, 1] = grad_query.astype(jnp.bfloat16)
            return carry

        lax.fori_loop(0, GROUP, one_span, 0)
        for distance in range(GROUP):
            spot = across(jnp.int32(distance))
            halo_out[parity, distance, 0] = value_acc[parity, spot].astype(jnp.bfloat16)
            halo_out[parity, distance, 1] = key_acc[parity, spot].astype(jnp.bfloat16)
            grad_key = key_acc[parity, GROUP + spot]
            add_inner(distance, 2, grad_key * taken[head, distance, 1].astype(jnp.float32))
            key_acc[parity, GROUP + spot] = own_acc[spot] + stats[distance][:, 1:2] * grad_key

    def step(index, carry):
        @pl.when(index < heads)
        def _():
            own(index).wait()
            for d in range(1, GROUP):
                take(index, d).wait_recv()

            @pl.when(not_last == 1)
            def _():
                up(index).start()

            for ahead in (2, 3):

                @pl.when(2 * index + ahead < heads)
                def _():
                    start_take(2 * index + ahead)

            @pl.when(not_first == 0)
            def _():
                halo[index] = jnp.zeros(halo.shape[1:], halo.dtype)

        @pl.when(jnp.logical_and(index >= 1, index <= heads))
        def _():
            head = index - 1

            @pl.when(not_first == 1)
            def _():
                up(head).wait_recv()

            @pl.when(head >= BACK_SLOTS)
            def _():
                drain_sends(head - BACK_SLOTS)

            @pl.when(jnp.logical_and(head >= 2, not_first == 1))
            def _():
                down(head - 2).wait_send()

            attention(head)
            own_back(head).start()
            for d in range(1, GROUP):
                give(head, d).start()

            @pl.when(not_first == 1)
            def _():
                down(head).start()

        @pl.when(index >= 2)
        def _():
            head = index - 2
            parity = lax.rem(head, 2)
            slot_back = lax.rem(head, BACK_SLOTS)

            @pl.when(not_last == 1)
            def _():
                down(head).wait_recv()

            @pl.when(not_last == 0)
            def _():
                halo_back[head] = jnp.zeros(halo_back.shape[1:], halo_back.dtype)

            for distance in range(GROUP):
                spot = GROUP + across(jnp.int32(distance))
                later = halo_back[head, distance, 1].astype(jnp.float32)
                add_inner(distance, 2, later * taken[head, distance, 1].astype(jnp.float32))
                grad_key = key_acc[parity, spot] + stats[distance][:, 1:2] * later
                grad_value = value_acc[parity, spot] + halo_back[head, distance, 0].astype(jnp.float32)
                back[slot_back, distance, 2] = grad_key.astype(jnp.bfloat16)
                back[slot_back, distance, 3] = grad_value.astype(jnp.bfloat16)
            own_ctx(head).start()
            for d in range(1, GROUP):
                give_ctx(head, d).start()

        return carry

    lax.fori_loop(0, heads + 2, step, 0)
    for d in range(1, GROUP):
        inner_copy(d).start()

    def finish_head(head, carry):
        for d in range(1, GROUP):
            take(head, d).wait_send()
            give(head, d).wait_recv()
            give_ctx(head, d).wait_recv()

        @pl.when(not_last == 1)
        def _():
            up(head).wait_send()

        @pl.when(head >= heads - BACK_SLOTS)
        def _():
            drain_sends(head)

        @pl.when(jnp.logical_and(head >= heads - 2, not_first == 1))
        def _():
            down(head).wait_send()

        return carry

    lax.fori_loop(0, heads, finish_head, 0)
    total_inner = inner[0]
    for d in range(1, GROUP):
        stats_copy(d).wait_send()
        inner_copy(d).wait()
        total_inner = total_inner + inner_taken[d]
    inner_ref[...] = total_inner


def noisy_at(clean_ref, noise_ref, index, cols, keep, share):
    return keep * clean_ref[index, :, cols].astype(jnp.float32) + share * noise_ref[index, :, cols].astype(jnp.float32)


def finish_kernel(
    heads, place_ref, share_ref, clean_ref, noise_ref, gains_ref,
    sums_ref, sums_other_ref, inner_ref, inner_other_ref, home_ref, attended_ref, grads_ref
):
    keep, share = share_ref[0], share_ref[1]
    place = place_ref[0]
    inverse = lax.rsqrt((sums_ref[...] + sums_other_ref[...]) / D + epsilon)
    cube = inverse * inverse * ((inner_ref[...] + inner_other_ref[...]) / D)
    inverse_q = spread_lanes(inverse)[0]
    cube_q, cube_k, cube_clean = spread_lanes(cube)
    for distance in range(GROUP):
        for head in range(heads):
            cols = columns_at(place ^ distance, heads * HEAD_DIM, head * HEAD_DIM, HEAD_DIM)
            gain_q, gain_k = gains_ref[0:1, cols], gains_ref[1:2, cols]
            query = noisy_at(clean_ref, noise_ref, 0, cols, keep, share)
            key = noisy_at(clean_ref, noise_ref, 1, cols, keep, share)
            clean_key = clean_ref[1, :, cols].astype(jnp.float32)
            grad = [home_ref[head, distance, which].astype(jnp.float32) for which in range(1, 4)]
            grad_query = inverse_q * gain_q * grad[0] - query * cube_q
            attended_ref[:, cols] = home_ref[head, distance, 0]
            grads_ref[0, :, cols] = keep * grad_query
            grads_ref[1, :, cols] = gain_k * grad[1] - keep * (key * cube_k) - clean_key * cube_clean
            grads_ref[2, :, cols] = grad[2]


def on_group(clean_qkv, noise_qkv, timestep, gain_q, gain_k, attended_grad):
    rows, local_width = clean_qkv.shape[1:]
    heads = local_width // GROUP // HEAD_DIM
    layers = lax.axis_size("tm") // GROUP
    places = lax.rem(lax.axis_index("tm"), GROUP).astype(jnp.int32)[None]
    noise_share = noise_share_of(timestep[0])
    keep_share = 1.0 - noise_share
    shares = jnp.stack([keep_share, noise_share])
    gains = jnp.stack([gain_q, gain_k])

    smem = pl.BlockSpec(memory_space=pltpu.SMEM)
    params = pltpu.CompilerParams(vmem_limit_bytes=VMEM_LIMIT)
    grid = (rows // ROWS,)
    by_rows = lambda parts: pl.BlockSpec((parts, ROWS, local_width), lambda i: (0, i, 0))
    flat = lambda count: pl.BlockSpec((ROWS, count), lambda i: (i, 0))
    by_head = lambda parts: pl.BlockSpec((heads, GROUP, parts, ROWS, HEAD_DIM), lambda i: (0, 0, 0, i, 0))
    gain_spec = pl.BlockSpec((2, local_width), lambda i: (0, 0))
    lanes = jax.ShapeDtypeStruct((rows, 128), jnp.float32)

    sums = pl.pallas_call(
        sums_kernel,
        grid=(rows // (2 * ROWS),),
        in_specs=[smem] + [pl.BlockSpec((2, 2 * ROWS, local_width), lambda i: (0, i, 0))] * 2,
        out_specs=pl.BlockSpec((2 * ROWS, 128), lambda i: (i, 0)),
        out_shape=lanes,
        compiler_params=params,
        name="sums",
    )(shares, clean_qkv, noise_qkv)
    sums_other = other_core(sums)
    packed, stats = pl.pallas_call(
        functools.partial(pack_kernel, heads),
        grid=grid,
        in_specs=[smem, smem, by_rows(3), by_rows(3), flat(local_width), gain_spec, flat(128), flat(128)],
        out_specs=[by_head(6), flat(128)],
        out_shape=[jax.ShapeDtypeStruct((heads, GROUP, 6, rows, HEAD_DIM), jnp.bfloat16), lanes],
        compiler_params=params,
        name="pack",
    )(places, shares, clean_qkv, noise_qkv, attended_grad, gains, sums, sums_other)

    half = lambda *lead: pltpu.VMEM(lead + (rows, HEAD_DIM), jnp.bfloat16)
    full = lambda *lead: pltpu.VMEM(lead + (rows, HEAD_DIM), jnp.float32)
    copies = lambda *shape: pltpu.SemaphoreType.DMA(shape)
    home, inner = pl.pallas_call(
        functools.partial(exchange_kernel, heads, layers),
        in_specs=[pl.BlockSpec(memory_space=pl.ANY), pl.BlockSpec(memory_space=pltpu.VMEM)],
        out_specs=[pl.BlockSpec(memory_space=pl.ANY), pl.BlockSpec(memory_space=pltpu.VMEM)],
        out_shape=[jax.ShapeDtypeStruct((heads, GROUP, 4, rows, HEAD_DIM), jnp.bfloat16), lanes],
        scratch_shapes=[
            half(heads, GROUP, 6),
            half(heads, GROUP, 2),
            half(heads, GROUP, 2),
            half(BACK_SLOTS, GROUP, 4),
            half(2, GROUP, 2),
            full(GROUP),
            half(2 * GROUP),
            half(2 * GROUP),
            full(2, 2 * GROUP),
            full(2, 2 * GROUP),
            full(GROUP),
            full(GROUP),
            full(GROUP),
            copies(heads),
            copies(heads, GROUP), copies(heads, GROUP),
            copies(GROUP), copies(GROUP),
            copies(GROUP), copies(GROUP),
            copies(heads), copies(heads),
            copies(heads), copies(heads),
            copies(heads),
            copies(heads, GROUP), copies(heads, GROUP),
            copies(heads),
            copies(heads, GROUP), copies(heads, GROUP),
        ],
        compiler_params=pltpu.CompilerParams(
            vmem_limit_bytes=EXCHANGE_VMEM, collective_id=0, has_side_effects=True
        ),
        cost_estimate=pl.CostEstimate(
            flops=heads * 2 * 6 * GROUP * (CONTEXT + 1) * rows * rows * HEAD_DIM,
            bytes_accessed=heads * GROUP * 22 * rows * HEAD_DIM,
            transcendentals=heads * GROUP * (CONTEXT + 1) * rows * rows,
        ),
        name="exchange",
    )(packed, stats)

    inner_other = other_core(inner)
    attended, clean_grads = pl.pallas_call(
        functools.partial(finish_kernel, heads),
        grid=grid,
        in_specs=[smem, smem, by_rows(2), by_rows(2), gain_spec] + [flat(128)] * 4 + [by_head(4)],
        out_specs=[flat(local_width), by_rows(3)],
        out_shape=[
            jax.ShapeDtypeStruct((rows, local_width), jnp.bfloat16),
            jax.ShapeDtypeStruct((3, rows, local_width), jnp.float32),
        ],
        compiler_params=params,
        name="finish",
    )(places, shares, clean_qkv, noise_qkv, gains, sums, sums_other, inner, inner_other, home)
    return (attended, clean_grads)


def solution(mesh):
    placed = (
        P(None, "tm", "head"),
        P(None, "tm", "head"),
        P("tm"),
        P("head"),
        P("head"),
        P("tm", "head"),
    )
    heads_here = D // HEAD_DIM // mesh.shape["head"]
    grouped = mesh.shape["head"] == 2 and mesh.shape["tm"] % GROUP == 0 and heads_here % GROUP == 0
    return jax.shard_map(
        on_group if grouped else on_device,
        mesh=mesh,
        in_specs=placed,
        out_specs=(P("tm", "head"), P(None, "tm", "head")),
        check_vma=False,
    )
```
